256 devices in a mesh: len: 4 (over y_hi, core), eng: 64 (over z, y_lo, x).
Axes of the slice: x: 4, y: 4 (y_hi: 2, y_lo: 2; y = y_hi * 2 + y_lo), z: 8, core: 2. Of those that a mesh axis runs over, the one named last changes fastest.
Arguments:
- less_green: bfloat16 [4, 2048, 2, 128, 128], P('len', 'eng'), may hold values from -6 to 6
- greater_green: bfloat16 [4, 2048, 2, 128, 128], P('len', 'eng'), may hold values from -6 to 6
- coulomb: bfloat16 [4, 2, 128, 128], P('len'), may hold values from -0.3125 to 0.3125
Outputs:
- polarization: bfloat16 [4, 2048, 2, 128, 128], P('len', 'eng')
- screened: bfloat16 [4, 2048, 4, 128, 128], P('len', 'eng')
The draws below stay inside these ranges and needn't reach their ends.
All inputs are finite; a program needn't handle non-finite values.
Results may differ from the reference program's by a relative error of at most 0.0057.
Values may be sent and summed in bfloat16 or wider, within the bound.
No kernel may reach another device: no remote copies, remote signals or barrier semaphores. Data moves between devices by JAX's collectives and lax.ppermute only.
A program may use at most 128 MiB of HBM per device.

```python
import math
import jax
import jax.numpy as jnp
from jax import lax

B = 128
NB = 4
NE = 2048


def levels(own_key, shape, shards, least, top_value):
    gain = 1.0
    for dim, shards_of in shards:
        draws = jax.random.uniform(jax.random.fold_in(jax.random.fold_in(own_key, 6), dim), (shards_of,), jnp.float32, least / len(shards), top_value / len(shards))
        gain = gain * jnp.repeat(jnp.exp(draws), shape[dim] // shards_of).reshape((-1,) + (1,) * (len(shape) - 1 - dim))
    return gain


def bell_draw(stream_key, shape, scale, limit, pieces=(), dtype=jnp.bfloat16):
    gain = levels(stream_key, shape, pieces, -0.22, 0.18) if pieces else 1.0
    values = jax.random.normal(stream_key, shape, jnp.float32) * scale * gain
    return jnp.minimum(jnp.maximum(values, -limit), limit).astype(dtype)


def setup_inputs(seed: int = 0) -> dict:
    key_list = jax.random.split(jax.random.key(seed), 4)
    return {
        "less_green": bell_draw(key_list[0], (NB, NE, 2, B, B), 1.0, 6.0, ((0, 4), (1, 64))),
        "greater_green": bell_draw(key_list[1], (NB, NE, 2, B, B), 1.0, 6.0, ((0, 4), (1, 64))),
        "coulomb": bell_draw(key_list[2], (NB, 2, B, B), (3 * B) ** -0.5, 0.3125, ((0, 4),)),
    }


def correlate_rows(less_rows, greater_rows):
    energies = less_rows.shape[0]
    less_wave = less_rows[:, 0].astype(jnp.float32) + 1j * less_rows[:, 1].astype(jnp.float32)
    greater_wave = greater_rows[:, 0].astype(jnp.float32) + 1j * greater_rows[:, 1].astype(jnp.float32)
    less_spec = jnp.fft.fft(less_wave, n=2 * energies, axis=0)
    greater_spec = jnp.fft.fft(greater_wave, n=2 * energies, axis=0)
    summed = jnp.fft.ifft(less_spec * jnp.conj(greater_spec), axis=0)[:energies]
    factor = 1.0 / math.sqrt(energies)
    return jnp.stack((-jnp.imag(summed) * factor, jnp.real(summed) * factor), axis=1).astype(jnp.bfloat16)

def screen(padded_polar, framed):
    lower_p = padded_polar[:-2].astype(jnp.float32)
    own_p = padded_polar[1:-1].astype(jnp.float32)
    upper_p = padded_polar[2:].astype(jnp.float32)
    own_diag = framed[1:-1, 0].astype(jnp.float32)
    own_up = framed[1:-1, 1].astype(jnp.float32)
    prev_up = framed[:-2, 1].astype(jnp.float32)
    next_diag = framed[2:, 0].astype(jnp.float32)
    from_lower = jnp.einsum('rji,recjk->recik', prev_up, lower_p).astype(jnp.bfloat16).astype(jnp.float32)
    from_own = jnp.einsum('rij,recjk->recik', own_diag, own_p).astype(jnp.bfloat16).astype(jnp.float32)
    from_upper = jnp.einsum('rij,recjk->recik', own_up, upper_p).astype(jnp.bfloat16).astype(jnp.float32)
    diag_block = jnp.einsum('recij,rjk->recik', from_lower, prev_up) + jnp.einsum('recij,rjk->recik', from_own, own_diag) + jnp.einsum('recij,rkj->recik', from_upper, own_up)
    upper_block = jnp.einsum('recij,rjk->recik', from_own, own_up) + jnp.einsum('recij,rjk->recik', from_upper, next_diag)
    return jnp.concatenate((diag_block, upper_block), axis=2).astype(jnp.bfloat16)

def reference(less_green, greater_green, coulomb):
    group = 8

    def regroup(green):
        moved = jnp.transpose(green.reshape(NB, NE, 2, B // group, group, B), (0, 3, 1, 2, 4, 5))
        return moved.reshape(NB * (B // group), NE, 2, group, B)
    polar_groups = lax.map(lambda pair: correlate_rows(pair[0], pair[1]), (regroup(less_green), regroup(greater_green)))
    polar_groups = polar_groups.reshape(NB, B // group, NE, 2, group, B)
    polarization = jnp.transpose(polar_groups, (0, 2, 3, 1, 4, 5)).reshape(NB, NE, 2, B, B)
    padded_polar = jnp.pad(polarization, ((1, 1), (0, 0), (0, 0), (0, 0), (0, 0)))
    framed = jnp.pad(coulomb, ((1, 1), (0, 0), (0, 0), (0, 0)))
    span = 16
    screened = jnp.zeros((NB, NE, 4, B, B), jnp.bfloat16)

    def step_block(index, result):
        start = (index * span).astype(jnp.int32)
        window = lax.dynamic_slice_in_dim(padded_polar, start, span, 1)
        block = screen(window, framed)
        return lax.dynamic_update_slice_in_dim(result, block, start, 1)
    screened = lax.fori_loop(0, NE // span, step_block, screened)
    return (polarization, screened)
```

```python
import math

import jax
import jax.numpy as jnp
import ml_dtypes
import numpy as np
from jax import lax
from jax.experimental import pallas as pl
from jax.experimental.pallas import tpu as pltpu
from jax.sharding import PartitionSpec as P

F32 = jnp.float32
BF16 = jnp.bfloat16

ENERGIES = 2048
SLOTS = 64
LOCAL = ENERGIES // SLOTS
SIDE = 128
HALF = SIDE // SLOTS
OUTER = 2 * SLOTS
MIB = 1024 * 1024


def halves(table):
    high = table.astype(np.float32).astype(ml_dtypes.bfloat16)
    low = (table - high.astype(np.float64)).astype(np.float32).astype(ml_dtypes.bfloat16)
    return high, low


def real_form(table):
    top = np.concatenate([table.real, -table.imag], axis=-1)
    bottom = np.concatenate([table.imag, table.real], axis=-1)
    return np.concatenate([top, bottom], axis=-2)


def dft_tables():
    period = 2 * ENERGIES
    outer = np.arange(OUTER)
    slow = np.arange(SLOTS)
    fast = np.arange(LOCAL)
    turn = 2j * np.pi
    first = real_form(np.exp(-turn * ((outer[:, None] * slow[None, :]) % OUTER) / OUTER))
    freq = outer[:, None, None] + OUTER * fast[None, :, None]
    phase = (freq * fast[None, None, :]) % period
    second = real_form(np.exp(-turn * phase / period))
    third = real_form(np.exp(turn * np.swapaxes(phase, 1, 2) / period))
    last = np.exp(turn * ((slow[:, None] * outer[None, :]) % OUTER) / OUTER)
    last = real_form(1j * last / (period * math.sqrt(ENERGIES)))
    first_hi, first_lo = halves(first)
    second_hi, second_lo = halves(second)
    third_hi, third_lo = halves(third)
    last_hi, last_lo = halves(last)
    return (
        np.concatenate([first_hi, first_lo], axis=1),
        np.concatenate([second_hi, second_lo, second_hi], axis=2),
        np.concatenate([third_hi, third_lo, third_hi], axis=2),
        np.concatenate([last_hi, last_lo], axis=0),
    )


TABLES = dft_tables()


def split(values):
    high = values.astype(BF16)
    return high, (values - high.astype(F32)).astype(BF16)


def mm(left, right):
    return jnp.dot(left, right, preferred_element_type=F32)


def pack_kernel(in_ref, out_ref, wide):
    def fill(n, carry):
        for part in range(2):
            start = pl.multiple_of((part * LOCAL + n) * SLOTS, SLOTS)
            wide[pl.ds(start, SLOTS), :] = in_ref[0, n, part].astype(F32)
        return carry

    def emit(row, carry):
        out_ref[row, 0] = wide[pl.ds(row, 2 * LOCAL, stride=SLOTS), :].astype(BF16)
        return carry

    lax.fori_loop(0, LOCAL, fill, 0, unroll=4)
    lax.fori_loop(0, SLOTS, emit, 0, unroll=4)


def pack(green):
    return pl.pallas_call(
        pack_kernel,
        grid=(HALF,),
        out_shape=jax.ShapeDtypeStruct((SLOTS, HALF, 2 * LOCAL, SIDE), BF16),
        in_specs=[pl.BlockSpec((1, LOCAL, 2, SLOTS, SIDE), lambda c: (0, 0, 0, c, 0))],
        out_specs=pl.BlockSpec((SLOTS, 1, 2 * LOCAL, SIDE), lambda c: (0, c, 0, 0)),
        scratch_shapes=[pltpu.VMEM((2 * LOCAL * SLOTS, SIDE), F32)],
        compiler_params=pltpu.CompilerParams(vmem_limit_bytes=24 * MIB),
        name="pack",
    )(green)


def unpack_kernel(in_ref, out_ref, wide):
    def fill(row, carry):
        start = pl.multiple_of(row * 2 * LOCAL, 2 * LOCAL)
        wide[pl.ds(start, 2 * LOCAL), :] = in_ref[row, 0].astype(F32)
        return carry

    def emit(n, carry):
        for part in range(2):
            line = wide[pl.ds(part * LOCAL + n, SLOTS, stride=2 * LOCAL), :]
            out_ref[0, n, part] = line.astype(BF16)
        return carry

    lax.fori_loop(0, SLOTS, fill, 0, unroll=4)
    lax.fori_loop(0, LOCAL, emit, 0, unroll=4)


def unpack(parcels):
    return pl.pallas_call(
        unpack_kernel,
        grid=(HALF,),
        out_shape=jax.ShapeDtypeStruct((1, LOCAL, 2, SIDE, SIDE), BF16),
        in_specs=[pl.BlockSpec((SLOTS, 1, 2 * LOCAL, SIDE), lambda c: (0, c, 0, 0))],
        out_specs=pl.BlockSpec((1, LOCAL, 2, SLOTS, SIDE), lambda c: (0, 0, 0, c, 0)),
        scratch_shapes=[pltpu.VMEM((2 * LOCAL * SLOTS, SIDE), F32)],
        compiler_params=pltpu.CompilerParams(vmem_limit_bytes=24 * MIB),
        name="unpack",
    )(parcels)


def correlate_kernel(g_ref, h_ref, w1_ref, w2_ref, w3_ref, w4_ref, out_ref, wide, mid, back, tail):
    chunk = 2 * LOCAL

    def fill(source, carry):
        start = pl.multiple_of(source * chunk, chunk)
        wide[0, pl.ds(start, chunk), :] = g_ref[source, 0].astype(F32)
        wide[1, pl.ds(start, chunk), :] = h_ref[source, 0].astype(F32)
        return carry

    def first(n, carry):
        cols = [
            jnp.concatenate(
                [
                    wide[which, pl.ds(part * LOCAL + n, SLOTS, stride=chunk), :]
                    for part in range(2)
                ],
                axis=0,
            ).astype(BF16)
            for which in range(2)
        ]
        x = jnp.concatenate(cols, axis=1)
        y = mm(w1_ref[...], jnp.concatenate([x, x], axis=0))
        start = pl.multiple_of(n * 2 * OUTER, 2 * OUTER)
        mid[0, pl.ds(start, 2 * OUTER), :] = y[:, :SIDE]
        mid[1, pl.ds(start, 2 * OUTER), :] = y[:, SIDE:]
        return carry

    def middle(k, carry):
        cols = [
            jnp.concatenate(
                [
                    mid[which, pl.ds(part * OUTER + k, LOCAL, stride=2 * OUTER), :]
                    for part in range(2)
                ],
                axis=0,
            )
            for which in range(2)
        ]
        high, low = split(jnp.concatenate(cols, axis=1))
        z = mm(w2_ref[k], jnp.concatenate([high, high, low], axis=0))
        g_re, g_im = z[:LOCAL, :SIDE], z[LOCAL:, :SIDE]
        h_re, h_im = z[:LOCAL, SIDE:], z[LOCAL:, SIDE:]
        product = jnp.concatenate([g_re * h_re + g_im * h_im, g_im * h_re - g_re * h_im], axis=0)
        high, low = split(product)
        start = pl.multiple_of(k * chunk, chunk)
        back[pl.ds(start, chunk), :] = mm(w3_ref[k], jnp.concatenate([high, high, low], axis=0))
        return carry

    def last(pair, carry):
        lines = [
            jnp.concatenate(
                [
                    back[pl.ds(part * LOCAL + 2 * pair + which, OUTER, stride=chunk), :]
                    for part in range(2)
                ],
                axis=0,
            )
            for which in range(2)
        ]
        high, low = split(jnp.concatenate(lines, axis=1))
        both = mm(w4_ref[...], high)
        y = both[:OUTER] + both[OUTER:] + mm(w4_ref[:OUTER, :], low)
        start = pl.multiple_of(pair * 2 * OUTER, 2 * OUTER)
        tail[pl.ds(start, OUTER), :] = y[:, :SIDE]
        tail[pl.ds(start + OUTER, OUTER), :] = y[:, SIDE:]
        return carry

    def emit(slot, carry):
        for part in range(2):
            line = tail[pl.ds(part * SLOTS + slot, LOCAL, stride=OUTER), :]
            out_ref[slot, 0, part * LOCAL : (part + 1) * LOCAL, :] = line.astype(BF16)
        return carry

    lax.fori_loop(0, SLOTS, fill, 0, unroll=4)
    lax.fori_loop(0, LOCAL, first, 0, unroll=2)
    lax.fori_loop(0, OUTER, middle, 0, unroll=4)
    lax.fori_loop(0, LOCAL // 2, last, 0, unroll=2)
    lax.fori_loop(0, SLOTS, emit, 0, unroll=4)


def correlate(less, greater, tables):
    parcel = pl.BlockSpec((SLOTS, 1, 2 * LOCAL, SIDE), lambda c: (0, c, 0, 0))
    whole = [
        pl.BlockSpec(t.shape, lambda c, rank=t.ndim: (0,) * rank, pipeline_mode=pl.Buffered(1))
        for t in tables
    ]
    return pl.pallas_call(
        correlate_kernel,
        grid=(HALF,),
        out_shape=jax.ShapeDtypeStruct((SLOTS, HALF, 2 * LOCAL, SIDE), BF16),
        in_specs=[parcel, parcel, *whole],
        out_specs=parcel,
        scratch_shapes=[
            pltpu.VMEM((2, ENERGIES * 2, SIDE), F32),
            pltpu.VMEM((2, LOCAL * 2 * OUTER, SIDE), F32),
            pltpu.VMEM((OUTER * 2 * LOCAL, SIDE), F32),
            pltpu.VMEM((LOCAL * OUTER, SIDE), F32),
        ],
        compiler_params=pltpu.CompilerParams(vmem_limit_bytes=52 * MIB),
        name="correlate",
    )(less, greater, *tables)


SPAN = 8


def screen_kernel(lower_ref, own_ref, upper_ref, left_ref, right_ref, out_ref):
    def step(n, carry):
        fields = []
        for which, ref in enumerate((lower_ref, own_ref, upper_ref)):
            both = jnp.concatenate([ref[0, n, 0], ref[0, n, 1]], axis=1)
            fields.append(mm(left_ref[which], both).astype(BF16))
        for part in range(2):
            cols = slice(part * SIDE, (part + 1) * SIDE)
            row = jnp.concatenate([field[:, cols] for field in fields], axis=1)
            result = mm(row, right_ref[...]).astype(BF16)
            out_ref[0, n, part] = result[:, :SIDE]
            out_ref[0, n, 2 + part] = result[:, SIDE:]
        return carry

    lax.fori_loop(0, SPAN, step, 0, unroll=2)


def screen(lower, own, upper, left, right):
    field = pl.BlockSpec((1, SPAN, 2, SIDE, SIDE), lambda s: (0, s, 0, 0, 0))
    return pl.pallas_call(
        screen_kernel,
        grid=(LOCAL // SPAN,),
        out_shape=jax.ShapeDtypeStruct((1, LOCAL, 4, SIDE, SIDE), BF16),
        in_specs=[
            field,
            field,
            field,
            pl.BlockSpec(left.shape, lambda s: (0, 0, 0)),
            pl.BlockSpec(right.shape, lambda s: (0, 0)),
        ],
        out_specs=pl.BlockSpec((1, SPAN, 4, SIDE, SIDE), lambda s: (0, s, 0, 0, 0)),
        compiler_params=pltpu.CompilerParams(vmem_limit_bytes=32 * MIB),
        name="screen",
    )(lower, own, upper, left, right)


def from_below(cells):
    ends = lax.axis_size("len") - 1
    return lax.ppermute(cells, "len", [(i, i + 1) for i in range(ends)])


def from_above(cells):
    ends = lax.axis_size("len") - 1
    return lax.ppermute(cells, "len", [(i + 1, i) for i in range(ends)])


def exchange(parcels):
    return lax.all_to_all(parcels, "eng", split_axis=0, concat_axis=0, tiled=True)


def coefficients(coulomb):
    own_diag, own_up = coulomb[0, 0], coulomb[0, 1]
    prev_up = from_below(coulomb[:, 1])[0]
    next_diag = from_above(coulomb[:, 0])[0]
    left = jnp.stack([prev_up.T, own_diag, own_up])
    right = jnp.concatenate(
        [
            jnp.concatenate([prev_up, jnp.zeros_like(prev_up)], axis=1),
            jnp.concatenate([own_diag, own_up], axis=1),
            jnp.concatenate([own_up.T, next_diag], axis=1),
        ],
        axis=0,
    )
    return left, right


def body(less_green, greater_green, coulomb):
    left, right = coefficients(coulomb)
    tables = [jnp.asarray(table) for table in TABLES]
    less = exchange(pack(less_green))
    greater = exchange(pack(greater_green))
    polar = unpack(exchange(correlate(less, greater, tables)))
    screened = screen(from_below(polar), polar, from_above(polar), left, right)
    return polar, screened


def solution(mesh):
    in_specs = (
        P("len", "eng", None, None, None),
        P("len", "eng", None, None, None),
        P("len", None, None, None),
    )
    out_specs = (P("len", "eng", None, None, None), P("len", "eng", None, None, None))
    return jax.shard_map(body, mesh=mesh, in_specs=in_specs, out_specs=out_specs, check_vma=False)
```

```python
import math

import jax
import jax.numpy as jnp
import ml_dtypes
import numpy as np
from jax import lax
from jax.experimental import pallas as pl
from jax.experimental.pallas import tpu as pltpu
from jax.sharding import PartitionSpec as P

F32 = jnp.float32
BF16 = jnp.bfloat16

ENERGIES = 2048
SLOTS = 64
LOCAL = ENERGIES // SLOTS
SIDE = 128
HALF = SIDE // SLOTS
OUTER = 2 * SLOTS
MIB = 1024 * 1024


def halves(table):
    high = table.astype(np.float32).astype(ml_dtypes.bfloat16)
    low = (table - high.astype(np.float64)).astype(np.float32).astype(ml_dtypes.bfloat16)
    return high, low


def real_form(table):
    top = np.concatenate([table.real, -table.imag], axis=-1)
    bottom = np.concatenate([table.imag, table.real], axis=-1)
    return np.concatenate([top, bottom], axis=-2)


def dft_tables():
    period = 2 * ENERGIES
    outer = np.arange(OUTER)
    slow = np.arange(SLOTS)
    fast = np.arange(LOCAL)
    turn = 2j * np.pi
    first = real_form(np.exp(-turn * ((outer[:, None] * slow[None, :]) % OUTER) / OUTER))
    freq = outer[:, None, None] + OUTER * fast[None, :, None]
    phase = (freq * fast[None, None, :]) % period
    second = real_form(np.exp(-turn * phase / period))
    third = real_form(np.exp(turn * np.swapaxes(phase, 1, 2) / period))
    last = np.exp(turn * ((slow[:, None] * outer[None, :]) % OUTER) / OUTER)
    last = real_form(1j * last / (period * math.sqrt(ENERGIES)))
    first_hi, first_lo = halves(first)
    second_hi, second_lo = halves(second)
    third_hi, third_lo = halves(third)
    last_hi, last_lo = halves(last)
    return (
        np.concatenate([first_hi, first_lo], axis=1),
        np.concatenate([second_hi, second_lo, second_hi], axis=2),
        np.concatenate([third_hi, third_lo, third_hi], axis=2),
        np.concatenate([last_hi, last_lo], axis=0),
    )


TABLES = dft_tables()


def split(values):
    high = values.astype(BF16)
    return high, (values - high.astype(F32)).astype(BF16)


def mm(left, right):
    return jnp.dot(left, right, preferred_element_type=F32)


def pack_kernel(less_ref, greater_ref, out_ref, wide):
    count = less_ref.shape[1]

    def fill(n, carry):
        for which, ref in enumerate((less_ref, greater_ref)):
            for part in range(2):
                start = pl.multiple_of(((which * 2 + part) * count + n) * SLOTS, SLOTS)
                wide[pl.ds(start, SLOTS), :] = ref[0, n, part].astype(F32)
        return carry

    def emit(row, carry):
        for which in range(2):
            for part in range(2):
                start = (which * 2 + part) * count * SLOTS + row
                line = wide[pl.ds(start, count, stride=SLOTS), :]
                out_ref[row, which, part] = line.astype(BF16)
        return carry

    lax.fori_loop(0, count, fill, 0, unroll=4)
    lax.fori_loop(0, SLOTS, emit, 0, unroll=8)


def pack(less, greater, chunk):
    steps = 2
    count = LOCAL // steps
    field = pl.BlockSpec((1, count, 2, SLOTS, SIDE), lambda s: (0, s, 0, chunk, 0))
    return pl.pallas_call(
        pack_kernel,
        grid=(steps,),
        out_shape=jax.ShapeDtypeStruct((SLOTS, 2, 2, LOCAL, SIDE), BF16),
        in_specs=[field, field],
        out_specs=pl.BlockSpec((SLOTS, 2, 2, count, SIDE), lambda s: (0, 0, 0, s, 0)),
        scratch_shapes=[pltpu.VMEM((4 * count * SLOTS, SIDE), F32)],
        compiler_params=pltpu.CompilerParams(vmem_limit_bytes=60 * MIB),
        cost_estimate=pl.CostEstimate(flops=0, bytes_accessed=8 * MIB, transcendentals=0),
        name="pack",
    )(less, greater)


def unpack_kernel(in_ref, out_ref, wide):
    def fill(row, carry):
        start = pl.multiple_of(row * 2 * LOCAL, 2 * LOCAL)
        wide[pl.ds(start, 2 * LOCAL), :] = in_ref[row].astype(F32)
        return carry

    def emit(n, carry):
        for part in range(2):
            line = wide[pl.ds(part * LOCAL + n, SLOTS, stride=2 * LOCAL), :]
            out_ref[0, n, part] = line.astype(BF16)
        return carry

    lax.fori_loop(0, SLOTS, fill, 0, unroll=4)
    lax.fori_loop(0, LOCAL, emit, 0, unroll=4)


def unpack(parcels):
    return pl.pallas_call(
        unpack_kernel,
        out_shape=jax.ShapeDtypeStruct((1, LOCAL, 2, SLOTS, SIDE), BF16),
        scratch_shapes=[pltpu.VMEM((2 * LOCAL * SLOTS, SIDE), F32)],
        compiler_params=pltpu.CompilerParams(vmem_limit_bytes=24 * MIB),
        cost_estimate=pl.CostEstimate(flops=0, bytes_accessed=8 * MIB, transcendentals=0),
        name="unpack",
    )(parcels)


def correlate_kernel(in_ref, w1_ref, w2_ref, w3_ref, w4_ref, out_ref, wide, mid, back, tail):
    chunk = 2 * LOCAL

    def fill(source, carry):
        start = pl.multiple_of(source * chunk, chunk)
        for which in range(2):
            block = in_ref[source, which].reshape(chunk, SIDE)
            wide[which, pl.ds(start, chunk), :] = block.astype(F32)
        return carry

    def first(n, carry):
        cols = [
            jnp.concatenate(
                [
                    wide[which, pl.ds(part * LOCAL + n, SLOTS, stride=chunk), :]
                    for part in range(2)
                ],
                axis=0,
            ).astype(BF16)
            for which in range(2)
        ]
        x = jnp.concatenate(cols, axis=1)
        y = mm(w1_ref[...], jnp.concatenate([x, x], axis=0))
        start = pl.multiple_of(n * 2 * OUTER, 2 * OUTER)
        mid[0, pl.ds(start, 2 * OUTER), :] = y[:, :SIDE]
        mid[1, pl.ds(start, 2 * OUTER), :] = y[:, SIDE:]
        return carry

    def middle(k, carry):
        cols = [
            jnp.concatenate(
                [
                    mid[which, pl.ds(part * OUTER + k, LOCAL, stride=2 * OUTER), :]
                    for part in range(2)
                ],
                axis=0,
            )
            for which in range(2)
        ]
        high, low = split(jnp.concatenate(cols, axis=1))
        z = mm(w2_ref[k], jnp.concatenate([high, high, low], axis=0))
        g_re, g_im = z[:LOCAL, :SIDE], z[LOCAL:, :SIDE]
        h_re, h_im = z[:LOCAL, SIDE:], z[LOCAL:, SIDE:]
        product = jnp.concatenate([g_re * h_re + g_im * h_im, g_im * h_re - g_re * h_im], axis=0)
        high, low = split(product)
        start = pl.multiple_of(k * chunk, chunk)
        back[pl.ds(start, chunk), :] = mm(w3_ref[k], jnp.concatenate([high, high, low], axis=0))
        return carry

    def last(pair, carry):
        lines = [
            jnp.concatenate(
                [
                    back[pl.ds(part * LOCAL + 2 * pair + which, OUTER, stride=chunk), :]
                    for part in range(2)
                ],
                axis=0,
            )
            for which in range(2)
        ]
        high, low = split(jnp.concatenate(lines, axis=1))
        both = mm(w4_ref[...], high)
        y = both[:OUTER] + both[OUTER:] + mm(w4_ref[:OUTER, :], low)
        start = pl.multiple_of(pair * 2 * OUTER, 2 * OUTER)
        tail[pl.ds(start, OUTER), :] = y[:, :SIDE]
        tail[pl.ds(start + OUTER, OUTER), :] = y[:, SIDE:]
        return carry

    def emit(slot, carry):
        for part in range(2):
            line = tail[pl.ds(part * SLOTS + slot, LOCAL, stride=OUTER), :]
            out_ref[slot, part * LOCAL : (part + 1) * LOCAL, :] = line.astype(BF16)
        return carry

    lax.fori_loop(0, SLOTS, fill, 0, unroll=4)
    lax.fori_loop(0, LOCAL, first, 0, unroll=U1)
    lax.fori_loop(0, OUTER, middle, 0, unroll=U2)
    lax.fori_loop(0, LOCAL // 2, last, 0, unroll=U4)
    lax.fori_loop(0, SLOTS, emit, 0, unroll=8)


U1, U2, U4 = 8, 32, 8


def correlate(parcels, tables):
    return pl.pallas_call(
        correlate_kernel,
        out_shape=jax.ShapeDtypeStruct((SLOTS, 2 * LOCAL, SIDE), BF16),
        scratch_shapes=[
            pltpu.VMEM((2, ENERGIES * 2, SIDE), F32),
            pltpu.VMEM((2, LOCAL * 2 * OUTER, SIDE), F32),
            pltpu.VMEM((OUTER * 2 * LOCAL, SIDE), F32),
            pltpu.VMEM((LOCAL * OUTER, SIDE), F32),
        ],
        compiler_params=pltpu.CompilerParams(vmem_limit_bytes=60 * MIB),
        cost_estimate=pl.CostEstimate(
            flops=12 * 10**9, bytes_accessed=40 * MIB, transcendentals=0
        ),
        name="correlate",
    )(parcels, *tables)


SPAN = 8
GROUP = 4


def screen_kernel(*refs):
    left_ref, right_ref, out_ref, polar_ref = refs[6:]

    def step(group, carry):
        rows = []
        for inner in range(GROUP):
            n = group * GROUP + inner
            fields = []
            for which in range(3):
                top, bottom = refs[2 * which : 2 * which + 2]
                blocks = [
                    jnp.concatenate([top[0, n, part], bottom[0, n, part]], axis=0)
                    for part in range(2)
                ]
                if which == 1:
                    polar_ref[0, n, 0] = blocks[0]
                    polar_ref[0, n, 1] = blocks[1]
                both = jnp.concatenate(blocks, axis=1)
                fields.append(mm(left_ref[which], both).astype(BF16))
            for part in range(2):
                cols = slice(part * SIDE, (part + 1) * SIDE)
                rows.append(jnp.concatenate([field[:, cols] for field in fields], axis=1))
        result = mm(jnp.concatenate(rows, axis=0), right_ref[...]).astype(BF16)
        for inner in range(GROUP):
            for part in range(2):
                start = (2 * inner + part) * SIDE
                block = result[start : start + SIDE]
                out_ref[0, group * GROUP + inner, part] = block[:, :SIDE]
                out_ref[0, group * GROUP + inner, 2 + part] = block[:, SIDE:]
        return carry

    lax.fori_loop(0, SPAN // GROUP, step, 0, unroll=True)


def screen(one, own, two, left, right):
    field = pl.BlockSpec((1, SPAN, 2, SLOTS, SIDE), lambda s: (0, s, 0, 0, 0))
    return pl.pallas_call(
        screen_kernel,
        grid=(LOCAL // SPAN,),
        out_shape=[
            jax.ShapeDtypeStruct((1, LOCAL, 4, SIDE, SIDE), BF16),
            jax.ShapeDtypeStruct((1, LOCAL, 2, SIDE, SIDE), BF16),
        ],
        in_specs=[field] * 6
        + [
            pl.BlockSpec(left.shape, lambda s: (0, 0, 0)),
            pl.BlockSpec(right.shape, lambda s: (0, 0)),
        ],
        out_specs=[
            pl.BlockSpec((1, SPAN, 4, SIDE, SIDE), lambda s: (0, s, 0, 0, 0)),
            pl.BlockSpec((1, SPAN, 2, SIDE, SIDE), lambda s: (0, s, 0, 0, 0)),
        ],
        compiler_params=pltpu.CompilerParams(vmem_limit_bytes=60 * MIB),
        name="screen",
    )(*one, *own, *two, left, right)


def from_below(cells):
    ends = lax.axis_size("len") - 1
    return lax.ppermute(cells, "len", [(i, i + 1) for i in range(ends)])


def from_above(cells):
    ends = lax.axis_size("len") - 1
    return lax.ppermute(cells, "len", [(i + 1, i) for i in range(ends)])


def swap(cells, first):
    ends = lax.axis_size("len") - 1
    pairs = [(i, i + 1) for i in range(first, ends, 2)]
    return lax.ppermute(cells, "len", pairs + [(j, i) for i, j in pairs])


def exchange(parcels):
    return lax.all_to_all(parcels, "eng", split_axis=0, concat_axis=0, tiled=True)


def coefficients(coulomb):
    own_diag, own_up = coulomb[0, 0], coulomb[0, 1]
    prev_up = from_below(coulomb[:, 1])[0]
    next_diag = from_above(coulomb[:, 0])[0]
    below = (prev_up.T, jnp.concatenate([prev_up, jnp.zeros_like(prev_up)], axis=1))
    above = (own_up, jnp.concatenate([own_up.T, next_diag], axis=1))
    odd = lax.axis_index("len") % 2 == 1
    one, two = [
        [jnp.where(odd, x, y) for x, y in zip(*order)]
        for order in ((below, above), (above, below))
    ]
    left = jnp.stack([one[0], own_diag, two[0]])
    middle = jnp.concatenate([own_diag, own_up], axis=1)
    right = jnp.concatenate([one[1], middle, two[1]], axis=0)
    return left, right


def body(less_green, greater_green, coulomb):
    tables = [jnp.asarray(table) for table in TABLES]
    packed = [pack(less_green, greater_green, 0)]
    later = lax.optimization_barrier((less_green, greater_green, *coefficients(coulomb)))
    left, right = later[2:]
    packed.append(pack(later[0], later[1], 1))
    arrived = [exchange(parcels) for parcels in packed]
    returned = [exchange(correlate(parcels, tables)) for parcels in arrived]
    own = [unpack(parcels) for parcels in returned]
    one = [swap(rows, 0) for rows in own]
    two = [swap(rows, 1) for rows in own]
    screened, polar = screen(one, own, two, left, right)
    return polar, screened


def solution(mesh):
    in_specs = (
        P("len", "eng", None, None, None),
        P("len", "eng", None, None, None),
        P("len", None, None, None),
    )
    out_specs = (P("len", "eng", None, None, None), P("len", "eng", None, None, None))
    return jax.shard_map(body, mesh=mesh, in_specs=in_specs, out_specs=out_specs, check_vma=False)
```

```python
import math

import jax
import jax.numpy as jnp
import ml_dtypes
import numpy as np
from jax import lax
from jax.experimental import pallas as pl
from jax.experimental.pallas import tpu as pltpu
from jax.sharding import PartitionSpec as P

F32 = jnp.float32
BF16 = jnp.bfloat16

ENERGIES = 2048
SLOTS = 64
LOCAL = ENERGIES // SLOTS
SIDE = 128
HALF = SIDE // SLOTS
OUTER = 2 * SLOTS
MIB = 1024 * 1024


def halves(table):
    high = table.astype(np.float32).astype(ml_dtypes.bfloat16)
    low = (table - high.astype(np.float64)).astype(np.float32).astype(ml_dtypes.bfloat16)
    return high, low


def real_form(table):
    top = np.concatenate([table.real, -table.imag], axis=-1)
    bottom = np.concatenate([table.imag, table.real], axis=-1)
    return np.concatenate([top, bottom], axis=-2)


def dft_tables():
    period = 2 * ENERGIES
    outer = np.arange(OUTER)
    slow = np.arange(SLOTS)
    fast = np.arange(LOCAL)
    turn = 2j * np.pi
    first = real_form(np.exp(-turn * ((outer[:, None] * slow[None, :]) % OUTER) / OUTER))
    freq = outer[:, None, None] + OUTER * fast[None, :, None]
    phase = (freq * fast[None, None, :]) % period
    second = real_form(np.exp(-turn * phase / period))
    third = real_form(np.exp(turn * np.swapaxes(phase, 1, 2) / period))
    last = np.exp(turn * ((slow[:, None] * outer[None, :]) % OUTER) / OUTER)
    last = real_form(1j * last / (period * math.sqrt(ENERGIES)))
    first_hi, first_lo = halves(first)
    second_hi, second_lo = halves(second)
    third_hi, third_lo = halves(third)
    last_hi, last_lo = halves(last)
    return (
        np.concatenate([first_hi, first_lo], axis=1),
        np.concatenate([second_hi, second_lo, second_hi], axis=2),
        np.concatenate([third_hi, third_lo, third_hi], axis=2),
        np.concatenate([last_hi, last_lo], axis=0),
    )


TABLES = dft_tables()


def split(values):
    high = values.astype(BF16)
    return high, (values - high.astype(F32)).astype(BF16)


def mm(left, right):
    return jnp.dot(left, right, preferred_element_type=F32)


def pack_kernel(*refs):
    *in_refs, out_ref, wide = refs
    count = in_refs[0].shape[1]

    def fill(n, carry):
        for which, ref in enumerate(in_refs):
            for part in range(2):
                start = pl.multiple_of(((which * 2 + part) * count + n) * SLOTS, SLOTS)
                wide[pl.ds(start, SLOTS), :] = ref[0, n, part].astype(F32)
        return carry

    def emit(row, carry):
        for which in range(len(in_refs)):
            for part in range(2):
                start = (which * 2 + part) * count * SLOTS + row
                line = wide[pl.ds(start, count, stride=SLOTS), :]
                out_ref[row, which, part] = line.astype(BF16)
        return carry

    lax.fori_loop(0, count, fill, 0, unroll=4)
    lax.fori_loop(0, SLOTS, emit, 0, unroll=8)


def pack(fields, chunk):
    steps = 2
    count = LOCAL // steps
    total = len(fields)
    block = pl.BlockSpec((1, count, 2, SLOTS, SIDE), lambda s: (0, s, 0, chunk, 0))
    return pl.pallas_call(
        pack_kernel,
        grid=(steps,),
        out_shape=jax.ShapeDtypeStruct((SLOTS, total, 2, LOCAL, SIDE), BF16),
        in_specs=[block] * total,
        out_specs=pl.BlockSpec((SLOTS, total, 2, count, SIDE), lambda s: (0, 0, 0, s, 0)),
        scratch_shapes=[pltpu.VMEM((2 * total * count * SLOTS, SIDE), F32)],
        compiler_params=pltpu.CompilerParams(vmem_limit_bytes=60 * MIB),
        cost_estimate=pl.CostEstimate(
            flops=0, bytes_accessed=4 * total * MIB, transcendentals=0
        ),
        name="pack",
    )(*fields)


def unpack_kernel(in_ref, out_ref, *rest):
    *half_refs, wide = rest

    def fill(row, carry):
        start = pl.multiple_of(row * 2 * LOCAL, 2 * LOCAL)
        wide[pl.ds(start, 2 * LOCAL), :] = in_ref[row].astype(F32)
        return carry

    def emit_from(begin, half_ref):
        def emit(step, carry):
            n = begin + step
            for part in range(2):
                line = wide[pl.ds(part * LOCAL + n, SLOTS, stride=2 * LOCAL), :].astype(BF16)
                out_ref[0, n, part] = line
                if half_ref is not None:
                    half_ref[0, step, part] = line
            return carry

        return emit

    lax.fori_loop(0, SLOTS, fill, 0, unroll=4)
    half = LOCAL // 2
    for begin, half_ref in zip((0, half), half_refs or (None, None)):
        lax.fori_loop(0, half, emit_from(begin, half_ref), 0, unroll=4)


def unpack(parcels, in_halves):
    shape = jax.ShapeDtypeStruct((1, LOCAL, 2, SLOTS, SIDE), BF16)
    half = jax.ShapeDtypeStruct((1, LOCAL // 2, 2, SLOTS, SIDE), BF16)
    return pl.pallas_call(
        unpack_kernel,
        out_shape=[shape, half, half] if in_halves else [shape],
        scratch_shapes=[pltpu.VMEM((2 * LOCAL * SLOTS, SIDE), F32)],
        compiler_params=pltpu.CompilerParams(vmem_limit_bytes=24 * MIB),
        cost_estimate=pl.CostEstimate(flops=0, bytes_accessed=8 * MIB, transcendentals=0),
        name="unpack",
    )(parcels)


def correlate_kernel(*refs):
    in_refs, refs = refs[:-13], refs[-13:]
    w1_ref, w2_from, w3_from, w4_ref, out_ref, wide, mid, back, tail, w2_ref, w3_ref = refs[:-2]
    fetches = [
        pltpu.make_async_copy(w2_from, w2_ref, refs[-2]),
        pltpu.make_async_copy(w3_from, w3_ref, refs[-1]),
    ]
    for fetch in fetches:
        fetch.start()
    places = [(ref, inner) for ref in in_refs for inner in range(ref.shape[1])]
    chunk = 2 * LOCAL

    def fill(source, carry):
        start = pl.multiple_of(source * chunk, chunk)
        for which, (ref, inner) in enumerate(places):
            block = ref[source, inner].reshape(chunk, SIDE)
            wide[which, pl.ds(start, chunk), :] = block.astype(F32)
        return carry

    def first(n, carry):
        cols = [
            jnp.concatenate(
                [
                    wide[which, pl.ds(part * LOCAL + n, SLOTS, stride=chunk), :]
                    for part in range(2)
                ],
                axis=0,
            ).astype(BF16)
            for which in range(2)
        ]
        x = jnp.concatenate(cols, axis=1)
        y = mm(w1_ref[...], jnp.concatenate([x, x], axis=0))
        start = pl.multiple_of(n * 2 * OUTER, 2 * OUTER)
        mid[0, pl.ds(start, 2 * OUTER), :] = y[:, :SIDE]
        mid[1, pl.ds(start, 2 * OUTER), :] = y[:, SIDE:]
        return carry

    def middle(k, carry):
        cols = [
            jnp.concatenate(
                [
                    mid[which, pl.ds(part * OUTER + k, LOCAL, stride=2 * OUTER), :]
                    for part in range(2)
                ],
                axis=0,
            )
            for which in range(2)
        ]
        high, low = split(jnp.concatenate(cols, axis=1))
        z = mm(w2_ref[k], jnp.concatenate([high, high, low], axis=0))
        g_re, g_im = z[:LOCAL, :SIDE], z[LOCAL:, :SIDE]
        h_re, h_im = z[:LOCAL, SIDE:], z[LOCAL:, SIDE:]
        product = jnp.concatenate([g_re * h_re + g_im * h_im, g_im * h_re - g_re * h_im], axis=0)
        high, low = split(product)
        start = pl.multiple_of(k * chunk, chunk)
        back[pl.ds(start, chunk), :] = mm(w3_ref[k], jnp.concatenate([high, high, low], axis=0))
        return carry

    def last(pair, carry):
        lines = [
            jnp.concatenate(
                [
                    back[pl.ds(part * LOCAL + 2 * pair + which, OUTER, stride=chunk), :]
                    for part in range(2)
                ],
                axis=0,
            )
            for which in range(2)
        ]
        high, low = split(jnp.concatenate(lines, axis=1))
        both = mm(w4_ref[...], high)
        y = both[:OUTER] + both[OUTER:] + mm(w4_ref[:OUTER, :], low)
        start = pl.multiple_of(pair * 2 * OUTER, 2 * OUTER)
        tail[pl.ds(start, OUTER), :] = y[:, :SIDE]
        tail[pl.ds(start + OUTER, OUTER), :] = y[:, SIDE:]
        return carry

    def emit(slot, carry):
        for part in range(2):
            line = tail[pl.ds(part * SLOTS + slot, LOCAL, stride=OUTER), :]
            out_ref[slot, part * LOCAL : (part + 1) * LOCAL, :] = line.astype(BF16)
        return carry

    lax.fori_loop(0, SLOTS, fill, 0, unroll=4)
    lax.fori_loop(0, LOCAL, first, 0, unroll=U1)
    for fetch in fetches:
        fetch.wait()
    lax.fori_loop(0, OUTER, middle, 0, unroll=U2)
    lax.fori_loop(0, LOCAL // 2, last, 0, unroll=U4)
    lax.fori_loop(0, SLOTS, emit, 0, unroll=8)


U1, U2, U4 = 8, 32, 8


def correlate(arrived, tables):
    vmem = pl.BlockSpec(memory_space=pltpu.VMEM)
    return pl.pallas_call(
        correlate_kernel,
        out_shape=jax.ShapeDtypeStruct((SLOTS, 2 * LOCAL, SIDE), BF16),
        in_specs=[vmem] * (len(arrived) + 1) + [pl.BlockSpec(memory_space=pl.ANY)] * 2 + [vmem],
        scratch_shapes=[
            pltpu.VMEM((2, ENERGIES * 2, SIDE), F32),
            pltpu.VMEM((2, LOCAL * 2 * OUTER, SIDE), F32),
            pltpu.VMEM((OUTER * 2 * LOCAL, SIDE), F32),
            pltpu.VMEM((LOCAL * OUTER, SIDE), F32),
            pltpu.VMEM(tables[1].shape, BF16),
            pltpu.VMEM(tables[2].shape, BF16),
            pltpu.SemaphoreType.DMA,
            pltpu.SemaphoreType.DMA,
        ],
        compiler_params=pltpu.CompilerParams(vmem_limit_bytes=60 * MIB),
        cost_estimate=pl.CostEstimate(
            flops=12 * 10**9, bytes_accessed=40 * MIB, transcendentals=0
        ),
        name="correlate",
    )(*arrived, *tables)


SPAN = 8
GROUP = 4


def screen_kernel(*refs):
    left_ref, right_ref = refs[6:8]
    out_ref, polar_ref = refs[-2:]

    def step(group, carry):
        rows = []
        for inner in range(GROUP):
            n = group * GROUP + inner
            fields = []
            for which in range(3):
                top, bottom = refs[2 * which : 2 * which + 2]
                blocks = [
                    jnp.concatenate([top[0, n, part], bottom[0, n, part]], axis=0)
                    for part in range(2)
                ]
                if which == 1:
                    polar_ref[0, n, 0] = blocks[0]
                    polar_ref[0, n, 1] = blocks[1]
                both = jnp.concatenate(blocks, axis=1)
                fields.append(mm(left_ref[which], both).astype(BF16))
            for part in range(2):
                cols = slice(part * SIDE, (part + 1) * SIDE)
                rows.append(jnp.concatenate([field[:, cols] for field in fields], axis=1))
        result = mm(jnp.concatenate(rows, axis=0), right_ref[...]).astype(BF16)
        for inner in range(GROUP):
            for part in range(2):
                start = (2 * inner + part) * SIDE
                block = result[start : start + SIDE]
                out_ref[0, group * GROUP + inner, part] = block[:, :SIDE]
                out_ref[0, group * GROUP + inner, 2 + part] = block[:, SIDE:]
        return carry

    lax.fori_loop(0, SPAN // GROUP, step, 0, unroll=True)


def screen(fields, left, right, half, results):
    steps = LOCAL // (2 * SPAN)

    def spec(parts):
        return pl.BlockSpec((1, SPAN, parts, SIDE, SIDE), lambda s: (0, s + half * steps, 0, 0, 0))

    def field_spec(field):
        first = half * steps if field.shape[1] == LOCAL else 0
        return pl.BlockSpec((1, SPAN, 2, SLOTS, SIDE), lambda s: (0, s + first, 0, 0, 0))

    return pl.pallas_call(
        screen_kernel,
        grid=(steps,),
        out_shape=[
            jax.ShapeDtypeStruct((1, LOCAL, 4, SIDE, SIDE), BF16),
            jax.ShapeDtypeStruct((1, LOCAL, 2, SIDE, SIDE), BF16),
        ],
        in_specs=[field_spec(field) for field in fields]
        + [
            pl.BlockSpec(left.shape, lambda s: (0, 0, 0)),
            pl.BlockSpec(right.shape, lambda s: (0, 0)),
        ]
        + [pl.BlockSpec(memory_space=pl.ANY)] * len(results),
        out_specs=[spec(4), spec(2)],
        input_output_aliases={8 + i: i for i in range(len(results))},
        compiler_params=pltpu.CompilerParams(vmem_limit_bytes=63 * MIB),
        cost_estimate=pl.CostEstimate(
            flops=2 * 10**9, bytes_accessed=10 * MIB, transcendentals=0
        ),
        name="screen",
    )(*fields, left, right, *results)


def from_below(cells):
    ends = lax.axis_size("len") - 1
    return lax.ppermute(cells, "len", [(i, i + 1) for i in range(ends)])


def from_above(cells):
    ends = lax.axis_size("len") - 1
    return lax.ppermute(cells, "len", [(i + 1, i) for i in range(ends)])


def swap(cells, first):
    ends = lax.axis_size("len") - 1
    pairs = [(i, i + 1) for i in range(first, ends, 2)]
    return lax.ppermute(cells, "len", pairs + [(j, i) for i, j in pairs])


def exchange(parcels):
    return lax.all_to_all(parcels, "eng", split_axis=0, concat_axis=0, tiled=True)


def coefficients(coulomb):
    own_diag, own_up = coulomb[0, 0], coulomb[0, 1]
    prev_up = from_below(coulomb[:, 1])[0]
    next_diag = from_above(coulomb[:, 0])[0]
    below = (prev_up.T, jnp.concatenate([prev_up, jnp.zeros_like(prev_up)], axis=1))
    above = (own_up, jnp.concatenate([own_up.T, next_diag], axis=1))
    odd = lax.axis_index("len") % 2 == 1
    one, two = [
        [jnp.where(odd, x, y) for x, y in zip(*order)]
        for order in ((below, above), (above, below))
    ]
    left = jnp.stack([one[0], own_diag, two[0]])
    middle = jnp.concatenate([own_diag, own_up], axis=1)
    right = jnp.concatenate([one[1], middle, two[1]], axis=0)
    return left, right


def forward(less, greater, tables, groups):
    arrived = [exchange(pack([(less, greater)[which] for which in group], 0)) for group in groups]
    second = exchange(pack([less, greater], 1))
    first = exchange(correlate(arrived, tables))
    return first, correlate([second], tables)


def body(less_green, greater_green, coulomb):
    tables = [jnp.asarray(table) for table in TABLES]
    first, second = lax.cond(
        lax.axis_index("len") % 2 == 0,
        lambda x, y: forward(x, y, tables, ((0, 1),)),
        lambda x, y: forward(x, y, tables, ((0,), (1,))),
        less_green,
        greater_green,
    )
    (top,) = unpack(first, False)
    top, left, right = lax.optimization_barrier((top, *coefficients(coulomb)))
    bottom, *halves = unpack(exchange(second), True)
    one = [swap(top, 0), swap(bottom, 0)]
    two = [swap(top, 1), *[swap(rows, 1) for rows in halves]]
    results = ()
    for half in range(2):
        fields = (*one, top, bottom, two[0], two[1 + half])
        results = screen(fields, left, right, half, results)
    screened, polar = results
    return polar, screened


def solution(mesh):
    in_specs = (
        P("len", "eng", None, None, None),
        P("len", "eng", None, None, None),
        P("len", None, None, None),
    )
    out_specs = (P("len", "eng", None, None, None), P("len", "eng", None, None, None))
    return jax.shard_map(body, mesh=mesh, in_specs=in_specs, out_specs=out_specs, check_vma=False)
```

```python
import math

import jax
import jax.numpy as jnp
import ml_dtypes
import numpy as np
from jax import lax
from jax.experimental import pallas as pl
from jax.experimental.pallas import tpu as pltpu
from jax.sharding import PartitionSpec as P

F32 = jnp.float32
BF16 = jnp.bfloat16

ENERGIES = 2048
SLOTS = 64
LOCAL = ENERGIES // SLOTS
SIDE = 128
HALF = SIDE // SLOTS
OUTER = 2 * SLOTS
MIB = 1024 * 1024


def halves(table):
    high = table.astype(np.float32).astype(ml_dtypes.bfloat16)
    low = (table - high.astype(np.float64)).astype(np.float32).astype(ml_dtypes.bfloat16)
    return high, low


def real_form(table):
    top = np.concatenate([table.real, -table.imag], axis=-1)
    bottom = np.concatenate([table.imag, table.real], axis=-1)
    return np.concatenate([top, bottom], axis=-2)


def dft_tables():
    period = 2 * ENERGIES
    outer = np.arange(OUTER)
    slow = np.arange(SLOTS)
    fast = np.arange(LOCAL)
    turn = 2j * np.pi
    first = real_form(np.exp(-turn * ((outer[:, None] * slow[None, :]) % OUTER) / OUTER))
    freq = outer[:, None, None] + OUTER * fast[None, :, None]
    phase = (freq * fast[None, None, :]) % period
    second = real_form(np.exp(-turn * phase / period))
    third = real_form(np.exp(turn * np.swapaxes(phase, 1, 2) / period))
    last = np.exp(turn * ((slow[:, None] * outer[None, :]) % OUTER) / OUTER)
    last = real_form(1j * last / (period * math.sqrt(ENERGIES)))
    first_hi, first_lo = halves(first)
    second_hi, second_lo = halves(second)
    third_hi, third_lo = halves(third)
    last_hi, last_lo = halves(last)
    return (
        np.concatenate([first_hi, first_lo], axis=1),
        np.concatenate([second_hi, second_lo, second_hi], axis=2),
        np.concatenate([third_hi, third_lo, third_hi], axis=2),
        np.concatenate([last_hi, last_lo], axis=0),
    )


TABLES = dft_tables()


def split(values):
    high = values.astype(BF16)
    return high, (values - high.astype(F32)).astype(BF16)


def mm(left, right):
    return jnp.dot(left, right, preferred_element_type=F32)


def pack_kernel(*refs):
    *in_refs, out_ref, wide = refs
    count = in_refs[0].shape[1]

    def fill(n, carry):
        for which, ref in enumerate(in_refs):
            for part in range(2):
                start = pl.multiple_of(((which * 2 + part) * count + n) * SLOTS, SLOTS)
                wide[pl.ds(start, SLOTS), :] = ref[0, n, part].astype(F32)
        return carry

    def emit(row, carry):
        for which in range(len(in_refs)):
            for part in range(2):
                start = (which * 2 + part) * count * SLOTS + row
                line = wide[pl.ds(start, count, stride=SLOTS), :]
                out_ref[row, which, part] = line.astype(BF16)
        return carry

    lax.fori_loop(0, count, fill, 0, unroll=4)
    lax.fori_loop(0, SLOTS, emit, 0, unroll=8)


def pack(pieces):
    steps = 2
    count = LOCAL // steps
    total = len(pieces)

    def block(chunk):
        return pl.BlockSpec((1, count, 2, SLOTS, SIDE), lambda s: (0, s, 0, chunk, 0))

    return pl.pallas_call(
        pack_kernel,
        grid=(steps,),
        out_shape=jax.ShapeDtypeStruct((SLOTS, total, 2, LOCAL, SIDE), BF16),
        in_specs=[block(chunk) for _, chunk in pieces],
        out_specs=pl.BlockSpec((SLOTS, total, 2, count, SIDE), lambda s: (0, 0, 0, s, 0)),
        scratch_shapes=[pltpu.VMEM((2 * total * count * SLOTS, SIDE), F32)],
        compiler_params=pltpu.CompilerParams(vmem_limit_bytes=60 * MIB),
        cost_estimate=pl.CostEstimate(
            flops=0, bytes_accessed=4 * total * MIB, transcendentals=0
        ),
        name="pack",
    )(*[field for field, _ in pieces])


def unpack_kernel(in_ref, out_ref, *rest):
    *half_refs, wide = rest

    def fill(row, carry):
        start = pl.multiple_of(row * 2 * LOCAL, 2 * LOCAL)
        wide[pl.ds(start, 2 * LOCAL), :] = in_ref[row].astype(F32)
        return carry

    def emit_from(begin, half_ref):
        def emit(step, carry):
            n = begin + step
            for part in range(2):
                line = wide[pl.ds(part * LOCAL + n, SLOTS, stride=2 * LOCAL), :].astype(BF16)
                out_ref[0, n, part] = line
                if half_ref is not None:
                    half_ref[0, step, part] = line
            return carry

        return emit

    lax.fori_loop(0, SLOTS, fill, 0, unroll=4)
    half = LOCAL // 2
    for begin, half_ref in zip((0, half), half_refs or (None, None)):
        lax.fori_loop(0, half, emit_from(begin, half_ref), 0, unroll=4)


def unpack(parcels, in_halves):
    shape = jax.ShapeDtypeStruct((1, LOCAL, 2, SLOTS, SIDE), BF16)
    half = jax.ShapeDtypeStruct((1, LOCAL // 2, 2, SLOTS, SIDE), BF16)
    return pl.pallas_call(
        unpack_kernel,
        out_shape=[shape, half, half] if in_halves else [shape],
        scratch_shapes=[pltpu.VMEM((2 * LOCAL * SLOTS, SIDE), F32)],
        compiler_params=pltpu.CompilerParams(vmem_limit_bytes=24 * MIB),
        cost_estimate=pl.CostEstimate(flops=0, bytes_accessed=8 * MIB, transcendentals=0),
        name="unpack",
    )(parcels)


def correlate_kernel(*refs):
    in_refs, refs = refs[:-13], refs[-13:]
    w1_ref, w2_from, w3_from, w4_ref, out_ref, wide, mid, back, tail, w2_ref, w3_ref = refs[:-2]
    fetches = [
        pltpu.make_async_copy(w2_from, w2_ref, refs[-2]),
        pltpu.make_async_copy(w3_from, w3_ref, refs[-1]),
    ]
    for fetch in fetches:
        fetch.start()
    chunk = 2 * LOCAL

    def fill(source, carry):
        start = pl.multiple_of(source * chunk, chunk)
        for which, ref in enumerate(in_refs):
            block = ref[source, 0].reshape(chunk, SIDE)
            wide[which, pl.ds(start, chunk), :] = block.astype(F32)
        return carry

    def first(n, carry):
        cols = [
            jnp.concatenate(
                [
                    wide[which, pl.ds(part * LOCAL + n, SLOTS, stride=chunk), :]
                    for part in range(2)
                ],
                axis=0,
            ).astype(BF16)
            for which in range(2)
        ]
        x = jnp.concatenate(cols, axis=1)
        y = mm(w1_ref[...], jnp.concatenate([x, x], axis=0))
        start = pl.multiple_of(n * 2 * OUTER, 2 * OUTER)
        mid[0, pl.ds(start, 2 * OUTER), :] = y[:, :SIDE]
        mid[1, pl.ds(start, 2 * OUTER), :] = y[:, SIDE:]
        return carry

    def middle(k, carry):
        cols = [
            jnp.concatenate(
                [
                    mid[which, pl.ds(part * OUTER + k, LOCAL, stride=2 * OUTER), :]
                    for part in range(2)
                ],
                axis=0,
            )
            for which in range(2)
        ]
        high, low = split(jnp.concatenate(cols, axis=1))
        z = mm(w2_ref[k], jnp.concatenate([high, high, low], axis=0))
        g_re, g_im = z[:LOCAL, :SIDE], z[LOCAL:, :SIDE]
        h_re, h_im = z[:LOCAL, SIDE:], z[LOCAL:, SIDE:]
        product = jnp.concatenate([g_re * h_re + g_im * h_im, g_im * h_re - g_re * h_im], axis=0)
        high, low = split(product)
        start = pl.multiple_of(k * chunk, chunk)
        back[pl.ds(start, chunk), :] = mm(w3_ref[k], jnp.concatenate([high, high, low], axis=0))
        return carry

    def last(pair, carry):
        lines = [
            jnp.concatenate(
                [
                    back[pl.ds(part * LOCAL + 2 * pair + which, OUTER, stride=chunk), :]
                    for part in range(2)
                ],
                axis=0,
            )
            for which in range(2)
        ]
        high, low = split(jnp.concatenate(lines, axis=1))
        both = mm(w4_ref[...], high)
        y = both[:OUTER] + both[OUTER:] + mm(w4_ref[:OUTER, :], low)
        start = pl.multiple_of(pair * 2 * OUTER, 2 * OUTER)
        tail[pl.ds(start, OUTER), :] = y[:, :SIDE]
        tail[pl.ds(start + OUTER, OUTER), :] = y[:, SIDE:]
        return carry

    def emit(slot, carry):
        for part in range(2):
            line = tail[pl.ds(part * SLOTS + slot, LOCAL, stride=OUTER), :]
            out_ref[slot, part * LOCAL : (part + 1) * LOCAL, :] = line.astype(BF16)
        return carry

    lax.fori_loop(0, SLOTS, fill, 0, unroll=4)
    lax.fori_loop(0, LOCAL, first, 0, unroll=U1)
    for fetch in fetches:
        fetch.wait()
    lax.fori_loop(0, OUTER, middle, 0, unroll=U2)
    lax.fori_loop(0, LOCAL // 2, last, 0, unroll=U4)
    lax.fori_loop(0, SLOTS, emit, 0, unroll=8)


U1, U2, U4 = 16, 32, 16


def correlate(less, greater, tables):
    def parcel(place):
        return pl.BlockSpec((SLOTS, 1, 2, LOCAL, SIDE), lambda s: (0, place, 0, 0, 0))

    vmem = pl.BlockSpec(memory_space=pltpu.VMEM)
    return pl.pallas_call(
        correlate_kernel,
        grid=(1,),
        out_shape=jax.ShapeDtypeStruct((SLOTS, 2 * LOCAL, SIDE), BF16),
        in_specs=[parcel(less[1]), parcel(greater[1]), vmem]
        + [pl.BlockSpec(memory_space=pl.ANY)] * 2
        + [vmem],
        scratch_shapes=[
            pltpu.VMEM((2, ENERGIES * 2, SIDE), F32),
            pltpu.VMEM((2, LOCAL * 2 * OUTER, SIDE), F32),
            pltpu.VMEM((OUTER * 2 * LOCAL, SIDE), F32),
            pltpu.VMEM((LOCAL * OUTER, SIDE), F32),
            pltpu.VMEM(tables[1].shape, BF16),
            pltpu.VMEM(tables[2].shape, BF16),
            pltpu.SemaphoreType.DMA,
            pltpu.SemaphoreType.DMA,
        ],
        compiler_params=pltpu.CompilerParams(vmem_limit_bytes=60 * MIB),
        cost_estimate=pl.CostEstimate(
            flops=12 * 10**9, bytes_accessed=40 * MIB, transcendentals=0
        ),
        name="correlate",
    )(less[0], greater[0], *tables)


SPAN = 8
GROUP = 4


def screen_kernel(*refs):
    left_ref, right_ref = refs[6:8]
    out_ref, polar_ref = refs[-2:]

    def step(group, carry):
        rows = []
        for inner in range(GROUP):
            n = group * GROUP + inner
            fields = []
            for which in range(3):
                top, bottom = refs[2 * which : 2 * which + 2]
                blocks = [
                    jnp.concatenate([top[0, n, part], bottom[0, n, part]], axis=0)
                    for part in range(2)
                ]
                if which == 1:
                    polar_ref[0, n, 0] = blocks[0]
                    polar_ref[0, n, 1] = blocks[1]
                both = jnp.concatenate(blocks, axis=1)
                fields.append(mm(left_ref[which], both).astype(BF16))
            for part in range(2):
                cols = slice(part * SIDE, (part + 1) * SIDE)
                rows.append(jnp.concatenate([field[:, cols] for field in fields], axis=1))
        result = mm(jnp.concatenate(rows, axis=0), right_ref[...]).astype(BF16)
        for inner in range(GROUP):
            for part in range(2):
                start = (2 * inner + part) * SIDE
                block = result[start : start + SIDE]
                out_ref[0, group * GROUP + inner, part] = block[:, :SIDE]
                out_ref[0, group * GROUP + inner, 2 + part] = block[:, SIDE:]
        return carry

    lax.fori_loop(0, SPAN // GROUP, step, 0, unroll=True)


def screen(fields, left, right, half, results):
    steps = LOCAL // (2 * SPAN)

    def spec(parts):
        return pl.BlockSpec((1, SPAN, parts, SIDE, SIDE), lambda s: (0, s + half * steps, 0, 0, 0))

    def field_spec(field):
        first = half * steps if field.shape[1] == LOCAL else 0
        return pl.BlockSpec((1, SPAN, 2, SLOTS, SIDE), lambda s: (0, s + first, 0, 0, 0))

    return pl.pallas_call(
        screen_kernel,
        grid=(steps,),
        out_shape=[
            jax.ShapeDtypeStruct((1, LOCAL, 4, SIDE, SIDE), BF16),
            jax.ShapeDtypeStruct((1, LOCAL, 2, SIDE, SIDE), BF16),
        ],
        in_specs=[field_spec(field) for field in fields]
        + [
            pl.BlockSpec(left.shape, lambda s: (0, 0, 0)),
            pl.BlockSpec(right.shape, lambda s: (0, 0)),
        ]
        + [pl.BlockSpec(memory_space=pl.ANY)] * len(results),
        out_specs=[spec(4), spec(2)],
        input_output_aliases={8 + i: i for i in range(len(results))},
        compiler_params=pltpu.CompilerParams(vmem_limit_bytes=63 * MIB),
        cost_estimate=pl.CostEstimate(
            flops=2 * 10**9, bytes_accessed=10 * MIB, transcendentals=0
        ),
        name="screen",
    )(*fields, left, right, *results)


def from_below(cells):
    ends = lax.axis_size("len") - 1
    return lax.ppermute(cells, "len", [(i, i + 1) for i in range(ends)])


def from_above(cells):
    ends = lax.axis_size("len") - 1
    return lax.ppermute(cells, "len", [(i + 1, i) for i in range(ends)])


def swap(cells, first):
    ends = lax.axis_size("len") - 1
    pairs = [(i, i + 1) for i in range(first, ends, 2)]
    return lax.ppermute(cells, "len", pairs + [(j, i) for i, j in pairs])


def exchange(parcels):
    return lax.all_to_all(parcels, "eng", split_axis=0, concat_axis=0, tiled=True)


def coefficients(coulomb):
    own_diag, own_up = coulomb[0, 0], coulomb[0, 1]
    prev_up = from_below(coulomb[:, 1])[0]
    next_diag = from_above(coulomb[:, 0])[0]
    below = (prev_up.T, jnp.concatenate([prev_up, jnp.zeros_like(prev_up)], axis=1))
    above = (own_up, jnp.concatenate([own_up.T, next_diag], axis=1))
    odd = lax.axis_index("len") % 2 == 1
    one, two = [
        [jnp.where(odd, x, y) for x, y in zip(*order)]
        for order in ((below, above), (above, below))
    ]
    left = jnp.stack([one[0], own_diag, two[0]])
    middle = jnp.concatenate([own_diag, own_up], axis=1)
    right = jnp.concatenate([one[1], middle, two[1]], axis=0)
    return left, right


def forward(less, greater, tables, ahead):
    sent = [(less, 0), (greater, 0), (less, 1), (greater, 1)]
    early = exchange(pack(sent[: 2 + ahead]))
    late = exchange(pack(sent[2 + ahead :]))
    first = exchange(correlate((early, 0), (early, 1), tables))
    second = correlate((early, 2) if ahead else (late, 0), (late, 1 - ahead), tables)
    return first, second


def body(less_green, greater_green, coulomb):
    tables = [jnp.asarray(table) for table in TABLES]
    first, second = lax.cond(
        lax.axis_index("len") % 2 == 0,
        lambda x, y: forward(x, y, tables, 0),
        lambda x, y: forward(x, y, tables, 1),
        less_green,
        greater_green,
    )
    (top,) = unpack(first, False)
    top, left, right = lax.optimization_barrier((top, *coefficients(coulomb)))
    bottom, *halves = unpack(exchange(second), True)
    one = [swap(top, 0), swap(bottom, 0)]
    two = [swap(top, 1), *[swap(rows, 1) for rows in halves]]
    results = ()
    for half in range(2):
        fields = (*one, top, bottom, two[0], two[1 + half])
        results = screen(fields, left, right, half, results)
    screened, polar = results
    return polar, screened


def solution(mesh):
    in_specs = (
        P("len", "eng", None, None, None),
        P("len", "eng", None, None, None),
        P("len", None, None, None),
    )
    out_specs = (P("len", "eng", None, None, None), P("len", "eng", None, None, None))
    return jax.shard_map(body, mesh=mesh, in_specs=in_specs, out_specs=out_specs, check_vma=False)
```

```python
import math

import jax
import jax.numpy as jnp
import ml_dtypes
import numpy as np
from jax import lax
from jax.experimental import pallas as pl
from jax.experimental.pallas import tpu as pltpu
from jax.sharding import PartitionSpec as P

F32 = jnp.float32
BF16 = jnp.bfloat16

ENERGIES = 2048
SLOTS = 64
LOCAL = ENERGIES // SLOTS
SIDE = 128
HALF = SIDE // SLOTS
OUTER = 2 * SLOTS
MIB = 1024 * 1024


def halves(table):
    high = table.astype(np.float32).astype(ml_dtypes.bfloat16)
    low = (table - high.astype(np.float64)).astype(np.float32).astype(ml_dtypes.bfloat16)
    return high, low


def real_form(table):
    top = np.concatenate([table.real, -table.imag], axis=-1)
    bottom = np.concatenate([table.imag, table.real], axis=-1)
    return np.concatenate([top, bottom], axis=-2)


def dft_tables():
    period = 2 * ENERGIES
    outer = np.arange(OUTER)
    slow = np.arange(SLOTS)
    fast = np.arange(LOCAL)
    turn = 2j * np.pi
    first = real_form(np.exp(-turn * ((outer[:, None] * slow[None, :]) % OUTER) / OUTER))
    freq = outer[:, None, None] + OUTER * fast[None, :, None]
    phase = (freq * fast[None, None, :]) % period
    second = real_form(np.exp(-turn * phase / period))
    third = real_form(np.exp(turn * np.swapaxes(phase, 1, 2) / period))
    last = np.exp(turn * ((slow[:, None] * outer[None, :]) % OUTER) / OUTER)
    last = real_form(1j * last / (period * math.sqrt(ENERGIES)))
    first_hi, first_lo = halves(first)
    second_hi, second_lo = halves(second)
    third_hi, third_lo = halves(third)
    last_hi, last_lo = halves(last)
    return (
        np.concatenate([first_hi, first_lo], axis=1),
        np.concatenate([second_hi, second_lo, second_hi], axis=2),
        np.concatenate([third_hi, third_lo, third_hi], axis=2),
        np.concatenate([last_hi, last_lo], axis=0),
    )


TABLES = dft_tables()


def split(values):
    high = values.astype(BF16)
    return high, (values - high.astype(F32)).astype(BF16)


def mm(left, right):
    return jnp.dot(left, right, preferred_element_type=F32)


def pack_kernel(*refs):
    *in_refs, out_ref, wide = refs
    count = in_refs[0].shape[1]

    def fill(n, carry):
        for which, ref in enumerate(in_refs):
            for part in range(2):
                start = pl.multiple_of(((which * 2 + part) * count + n) * SLOTS, SLOTS)
                wide[pl.ds(start, SLOTS), :] = ref[0, n, part].astype(F32)
        return carry

    def emit(row, carry):
        for which in range(len(in_refs)):
            for part in range(2):
                start = (which * 2 + part) * count * SLOTS + row
                line = wide[pl.ds(start, count, stride=SLOTS), :]
                out_ref[row, which, part] = line.astype(BF16)
        return carry

    lax.fori_loop(0, count, fill, 0, unroll=4)
    lax.fori_loop(0, SLOTS, emit, 0, unroll=8)


def pack(pieces):
    steps = 2
    count = LOCAL // steps
    total = len(pieces)

    def block(chunk):
        return pl.BlockSpec((1, count, 2, SLOTS, SIDE), lambda s: (0, s, 0, chunk, 0))

    return pl.pallas_call(
        pack_kernel,
        grid=(steps,),
        out_shape=jax.ShapeDtypeStruct((SLOTS, total, 2, LOCAL, SIDE), BF16),
        in_specs=[block(chunk) for _, chunk in pieces],
        out_specs=pl.BlockSpec((SLOTS, total, 2, count, SIDE), lambda s: (0, 0, 0, s, 0)),
        scratch_shapes=[pltpu.VMEM((2 * total * count * SLOTS, SIDE), F32)],
        compiler_params=pltpu.CompilerParams(vmem_limit_bytes=60 * MIB),
        cost_estimate=pl.CostEstimate(
            flops=0, bytes_accessed=4 * total * MIB, transcendentals=0
        ),
        name="pack",
    )(*[field for field, _ in pieces])


def unpack_kernel(in_ref, out_ref, *rest):
    *half_refs, wide = rest

    def fill(row, carry):
        start = pl.multiple_of(row * 2 * LOCAL, 2 * LOCAL)
        wide[pl.ds(start, 2 * LOCAL), :] = in_ref[row].astype(F32)
        return carry

    def emit_from(begin, half_ref):
        def emit(step, carry):
            n = begin + step
            for part in range(2):
                line = wide[pl.ds(part * LOCAL + n, SLOTS, stride=2 * LOCAL), :].astype(BF16)
                out_ref[0, n, part] = line
                if half_ref is not None:
                    half_ref[0, step, part] = line
            return carry

        return emit

    lax.fori_loop(0, SLOTS, fill, 0, unroll=4)
    half = LOCAL // 2
    for begin, half_ref in zip((0, half), half_refs or (None, None)):
        lax.fori_loop(0, half, emit_from(begin, half_ref), 0, unroll=4)


def unpack(parcels, in_halves):
    shape = jax.ShapeDtypeStruct((1, LOCAL, 2, SLOTS, SIDE), BF16)
    half = jax.ShapeDtypeStruct((1, LOCAL // 2, 2, SLOTS, SIDE), BF16)
    return pl.pallas_call(
        unpack_kernel,
        out_shape=[shape, half, half] if in_halves else [shape],
        scratch_shapes=[pltpu.VMEM((2 * LOCAL * SLOTS, SIDE), F32)],
        compiler_params=pltpu.CompilerParams(vmem_limit_bytes=24 * MIB),
        cost_estimate=pl.CostEstimate(flops=0, bytes_accessed=8 * MIB, transcendentals=0),
        name="unpack",
    )(parcels)


def correlate_kernel(*refs):
    in_refs, refs = refs[:-13], refs[-13:]
    w1_ref, w2_from, w3_from, w4_ref, out_ref, wide, mid, back, tail, w2_ref, w3_ref = refs[:-2]
    fetches = [
        pltpu.make_async_copy(w2_from, w2_ref, refs[-2]),
        pltpu.make_async_copy(w3_from, w3_ref, refs[-1]),
    ]
    for fetch in fetches:
        fetch.start()
    chunk = 2 * LOCAL

    def fill(source, carry):
        start = pl.multiple_of(source * chunk, chunk)
        for which, ref in enumerate(in_refs):
            block = ref[source, 0].reshape(chunk, SIDE)
            wide[which, pl.ds(start, chunk), :] = block.astype(F32)
        return carry

    def first(n, carry):
        cols = [
            jnp.concatenate(
                [
                    wide[which, pl.ds(part * LOCAL + n, SLOTS, stride=chunk), :]
                    for part in range(2)
                ],
                axis=0,
            ).astype(BF16)
            for which in range(2)
        ]
        x = jnp.concatenate(cols, axis=1)
        y = mm(w1_ref[...], jnp.concatenate([x, x], axis=0))
        start = pl.multiple_of(n * 2 * OUTER, 2 * OUTER)
        mid[0, pl.ds(start, 2 * OUTER), :] = y[:, :SIDE]
        mid[1, pl.ds(start, 2 * OUTER), :] = y[:, SIDE:]
        return carry

    def middle(k, carry):
        cols = [
            jnp.concatenate(
                [
                    mid[which, pl.ds(part * OUTER + k, LOCAL, stride=2 * OUTER), :]
                    for part in range(2)
                ],
                axis=0,
            )
            for which in range(2)
        ]
        high, low = split(jnp.concatenate(cols, axis=1))
        z = mm(w2_ref[k], jnp.concatenate([high, high, low], axis=0))
        g_re, g_im = z[:LOCAL, :SIDE], z[LOCAL:, :SIDE]
        h_re, h_im = z[:LOCAL, SIDE:], z[LOCAL:, SIDE:]
        product = jnp.concatenate([g_re * h_re + g_im * h_im, g_im * h_re - g_re * h_im], axis=0)
        high, low = split(product)
        start = pl.multiple_of(k * chunk, chunk)
        back[pl.ds(start, chunk), :] = mm(w3_ref[k], jnp.concatenate([high, high, low], axis=0))
        return carry

    def last(pair, carry):
        lines = [
            jnp.concatenate(
                [
                    back[pl.ds(part * LOCAL + 2 * pair + which, OUTER, stride=chunk), :]
                    for part in range(2)
                ],
                axis=0,
            )
            for which in range(2)
        ]
        high, low = split(jnp.concatenate(lines, axis=1))
        both = mm(w4_ref[...], high)
        y = both[:OUTER] + both[OUTER:] + mm(w4_ref[:OUTER, :], low)
        start = pl.multiple_of(pair * 2 * OUTER, 2 * OUTER)
        tail[pl.ds(start, OUTER), :] = y[:, :SIDE]
        tail[pl.ds(start + OUTER, OUTER), :] = y[:, SIDE:]
        return carry

    def emit(slot, carry):
        for part in range(2):
            line = tail[pl.ds(part * SLOTS + slot, LOCAL, stride=OUTER), :]
            out_ref[slot, part * LOCAL : (part + 1) * LOCAL, :] = line.astype(BF16)
        return carry

    lax.fori_loop(0, SLOTS, fill, 0, unroll=4)
    lax.fori_loop(0, LOCAL, first, 0, unroll=U1)
    for fetch in fetches:
        fetch.wait()
    lax.fori_loop(0, OUTER, middle, 0, unroll=U2)
    lax.fori_loop(0, LOCAL // 2, last, 0, unroll=U4)
    lax.fori_loop(0, SLOTS, emit, 0, unroll=8)


U1, U2, U4 = 16, 32, 16


def correlate(less, greater, tables):
    def parcel(place):
        return pl.BlockSpec((SLOTS, 1, 2, LOCAL, SIDE), lambda s: (0, place, 0, 0, 0))

    vmem = pl.BlockSpec(memory_space=pltpu.VMEM)
    return pl.pallas_call(
        correlate_kernel,
        grid=(1,),
        out_shape=jax.ShapeDtypeStruct((SLOTS, 2 * LOCAL, SIDE), BF16),
        in_specs=[parcel(less[1]), parcel(greater[1]), vmem]
        + [pl.BlockSpec(memory_space=pl.ANY)] * 2
        + [vmem],
        scratch_shapes=[
            pltpu.VMEM((2, ENERGIES * 2, SIDE), F32),
            pltpu.VMEM((2, LOCAL * 2 * OUTER, SIDE), F32),
            pltpu.VMEM((OUTER * 2 * LOCAL, SIDE), F32),
            pltpu.VMEM((LOCAL * OUTER, SIDE), F32),
            pltpu.VMEM(tables[1].shape, BF16),
            pltpu.VMEM(tables[2].shape, BF16),
            pltpu.SemaphoreType.DMA,
            pltpu.SemaphoreType.DMA,
        ],
        compiler_params=pltpu.CompilerParams(vmem_limit_bytes=60 * MIB),
        cost_estimate=pl.CostEstimate(
            flops=12 * 10**9, bytes_accessed=40 * MIB, transcendentals=0
        ),
        name="correlate",
    )(less[0], greater[0], *tables)


SPAN = 8
GROUP = 4


def screen_kernel(*refs):
    left_ref, right_ref = refs[6:8]
    out_ref, polar_ref = refs[-2:]

    def step(group, carry):
        rows = []
        for inner in range(GROUP):
            n = group * GROUP + inner
            fields = []
            for which in range(3):
                top, bottom = refs[2 * which : 2 * which + 2]
                blocks = [
                    jnp.concatenate([top[0, n, part], bottom[0, n, part]], axis=0)
                    for part in range(2)
                ]
                if which == 1:
                    polar_ref[0, n, 0] = blocks[0]
                    polar_ref[0, n, 1] = blocks[1]
                both = jnp.concatenate(blocks, axis=1)
                fields.append(mm(left_ref[which], both).astype(BF16))
            for part in range(2):
                cols = slice(part * SIDE, (part + 1) * SIDE)
                rows.append(jnp.concatenate([field[:, cols] for field in fields], axis=1))
        result = mm(jnp.concatenate(rows, axis=0), right_ref[...]).astype(BF16)
        for inner in range(GROUP):
            for part in range(2):
                start = (2 * inner + part) * SIDE
                block = result[start : start + SIDE]
                out_ref[0, group * GROUP + inner, part] = block[:, :SIDE]
                out_ref[0, group * GROUP + inner, 2 + part] = block[:, SIDE:]
        return carry

    lax.fori_loop(0, SPAN // GROUP, step, 0, unroll=True)


def screen(fields, left, right, half, results):
    steps = LOCAL // (2 * SPAN)

    def spec(parts):
        return pl.BlockSpec((1, SPAN, parts, SIDE, SIDE), lambda s: (0, s + half * steps, 0, 0, 0))

    def field_spec(field):
        first = half * steps if field.shape[1] == LOCAL else 0
        return pl.BlockSpec((1, SPAN, 2, SLOTS, SIDE), lambda s: (0, s + first, 0, 0, 0))

    return pl.pallas_call(
        screen_kernel,
        grid=(steps,),
        out_shape=[
            jax.ShapeDtypeStruct((1, LOCAL, 4, SIDE, SIDE), BF16),
            jax.ShapeDtypeStruct((1, LOCAL, 2, SIDE, SIDE), BF16),
        ],
        in_specs=[field_spec(field) for field in fields]
        + [
            pl.BlockSpec(left.shape, lambda s: (0, 0, 0)),
            pl.BlockSpec(right.shape, lambda s: (0, 0)),
        ]
        + [pl.BlockSpec(memory_space=pl.ANY)] * len(results),
        out_specs=[spec(4), spec(2)],
        input_output_aliases={8 + i: i for i in range(len(results))},
        compiler_params=pltpu.CompilerParams(vmem_limit_bytes=63 * MIB),
        cost_estimate=pl.CostEstimate(
            flops=2 * 10**9, bytes_accessed=10 * MIB, transcendentals=0
        ),
        name="screen",
    )(*fields, left, right, *results)


def from_below(cells):
    ends = lax.axis_size("len") - 1
    return lax.ppermute(cells, "len", [(i, i + 1) for i in range(ends)])


def from_above(cells):
    ends = lax.axis_size("len") - 1
    return lax.ppermute(cells, "len", [(i + 1, i) for i in range(ends)])


def swap(cells, first):
    ends = lax.axis_size("len") - 1
    pairs = [(i, i + 1) for i in range(first, ends, 2)]
    return lax.ppermute(cells, "len", pairs + [(j, i) for i, j in pairs])


def exchange(parcels):
    return lax.all_to_all(parcels, "eng", split_axis=0, concat_axis=0, tiled=True)


def coefficients(coulomb):
    own_diag, own_up = coulomb[0, 0], coulomb[0, 1]
    prev_up = from_below(coulomb[:, 1])[0]
    next_diag = from_above(coulomb[:, 0])[0]
    below = (prev_up.T, jnp.concatenate([prev_up, jnp.zeros_like(prev_up)], axis=1))
    above = (own_up, jnp.concatenate([own_up.T, next_diag], axis=1))
    odd = lax.axis_index("len") % 2 == 1
    one, two = [
        [jnp.where(odd, x, y) for x, y in zip(*order)]
        for order in ((below, above), (above, below))
    ]
    left = jnp.stack([one[0], own_diag, two[0]])
    middle = jnp.concatenate([own_diag, own_up], axis=1)
    right = jnp.concatenate([one[1], middle, two[1]], axis=0)
    return left, right


def forward(less, greater, tables, apart):
    if apart:
        pair = [(exchange(pack([(field, 0)])), 0) for field in (less, greater)]
    else:
        both = exchange(pack([(less, 0), (greater, 0)]))
        pair = [(both, 0), (both, 1)]
    late = exchange(pack([(less, 1), (greater, 1)]))
    first = exchange(correlate(*pair, tables))
    return first, correlate((late, 0), (late, 1), tables)


def body(less_green, greater_green, coulomb):
    tables = [jnp.asarray(table) for table in TABLES]
    first, second = lax.cond(
        lax.axis_index("len") % 2 == 0,
        lambda x, y: forward(x, y, tables, False),
        lambda x, y: forward(x, y, tables, True),
        less_green,
        greater_green,
    )
    (top,) = unpack(first, False)
    top, left, right = lax.optimization_barrier((top, *coefficients(coulomb)))
    bottom, *halves = unpack(exchange(second), True)
    one = [swap(top, 0), swap(bottom, 0)]
    two = [swap(top, 1), *[swap(rows, 1) for rows in halves]]
    results = ()
    for half in range(2):
        fields = (*one, top, bottom, two[0], two[1 + half])
        results = screen(fields, left, right, half, results)
    screened, polar = results
    return polar, screened


def solution(mesh):
    in_specs = (
        P("len", "eng", None, None, None),
        P("len", "eng", None, None, None),
        P("len", None, None, None),
    )
    out_specs = (P("len", "eng", None, None, None), P("len", "eng", None, None, None))
    return jax.shard_map(body, mesh=mesh, in_specs=in_specs, out_specs=out_specs, check_vma=False)
```

```python
import math

import jax
import jax.numpy as jnp
import ml_dtypes
import numpy as np
from jax import lax
from jax.experimental import pallas as pl
from jax.experimental.pallas import tpu as pltpu
from jax.sharding import PartitionSpec as P

F32 = jnp.float32
BF16 = jnp.bfloat16

ENERGIES = 2048
SLOTS = 64
LOCAL = ENERGIES // SLOTS
SIDE = 128
HALF = SIDE // SLOTS
OUTER = 2 * SLOTS
MIB = 1024 * 1024


def halves(table):
    high = table.astype(np.float32).astype(ml_dtypes.bfloat16)
    low = (table - high.astype(np.float64)).astype(np.float32).astype(ml_dtypes.bfloat16)
    return high, low


def real_form(table):
    top = np.concatenate([table.real, -table.imag], axis=-1)
    bottom = np.concatenate([table.imag, table.real], axis=-1)
    return np.concatenate([top, bottom], axis=-2)


def dft_tables():
    period = 2 * ENERGIES
    outer = np.arange(OUTER)
    slow = np.arange(SLOTS)
    fast = np.arange(LOCAL)
    turn = 2j * np.pi
    first = real_form(np.exp(-turn * ((outer[:, None] * slow[None, :]) % OUTER) / OUTER))
    freq = outer[:, None, None] + OUTER * fast[None, :, None]
    phase = (freq * fast[None, None, :]) % period
    second = real_form(np.exp(-turn * phase / period))
    third = real_form(np.exp(turn * np.swapaxes(phase, 1, 2) / period))
    last = np.exp(turn * ((slow[:, None] * outer[None, :]) % OUTER) / OUTER)
    last = real_form(1j * last / (period * math.sqrt(ENERGIES)))
    first_hi, first_lo = halves(first)
    second_hi, second_lo = halves(second)
    third_hi, third_lo = halves(third)
    last_hi, last_lo = halves(last)
    return (
        np.concatenate([first_hi, first_lo], axis=1),
        np.concatenate([second_hi, second_lo, second_hi], axis=2),
        np.concatenate([third_hi, third_lo, third_hi], axis=2),
        np.concatenate([last_hi, last_lo], axis=0),
    )


TABLES = dft_tables()


def split(values):
    high = values.astype(BF16)
    return high, (values - high.astype(F32)).astype(BF16)


def mm(left, right):
    return jnp.dot(left, right, preferred_element_type=F32)


def pack_kernel(*refs):
    *in_refs, out_ref, wide = refs
    count = in_refs[0].shape[1]

    def fill(n, carry):
        for which, ref in enumerate(in_refs):
            for part in range(2):
                start = pl.multiple_of(((which * 2 + part) * count + n) * SLOTS, SLOTS)
                wide[pl.ds(start, SLOTS), :] = ref[0, n, part].astype(F32)
        return carry

    def emit(row, carry):
        for which in range(len(in_refs)):
            for part in range(2):
                start = (which * 2 + part) * count * SLOTS + row
                line = wide[pl.ds(start, count, stride=SLOTS), :]
                out_ref[row, which, part] = line.astype(BF16)
        return carry

    lax.fori_loop(0, count, fill, 0, unroll=4)
    lax.fori_loop(0, SLOTS, emit, 0, unroll=8)


def pack(pieces):
    steps = 2
    count = LOCAL // steps
    total = len(pieces)

    def block(chunk):
        return pl.BlockSpec((1, count, 2, SLOTS, SIDE), lambda s: (0, s, 0, chunk, 0))

    return pl.pallas_call(
        pack_kernel,
        grid=(steps,),
        out_shape=jax.ShapeDtypeStruct((SLOTS, total, 2, LOCAL, SIDE), BF16),
        in_specs=[block(chunk) for _, chunk in pieces],
        out_specs=pl.BlockSpec((SLOTS, total, 2, count, SIDE), lambda s: (0, 0, 0, s, 0)),
        scratch_shapes=[pltpu.VMEM((2 * total * count * SLOTS, SIDE), F32)],
        compiler_params=pltpu.CompilerParams(vmem_limit_bytes=60 * MIB),
        cost_estimate=pl.CostEstimate(
            flops=0, bytes_accessed=4 * total * MIB, transcendentals=0
        ),
        name="pack",
    )(*[field for field, _ in pieces])


def unpack_kernel(in_ref, out_ref, *rest):
    *half_refs, wide = rest

    def fill(row, carry):
        start = pl.multiple_of(row * 2 * LOCAL, 2 * LOCAL)
        wide[pl.ds(start, 2 * LOCAL), :] = in_ref[row].astype(F32)
        return carry

    def emit_from(begin, half_ref):
        def emit(step, carry):
            n = begin + step
            for part in range(2):
                line = wide[pl.ds(part * LOCAL + n, SLOTS, stride=2 * LOCAL), :].astype(BF16)
                out_ref[0, n, part] = line
                if half_ref is not None:
                    half_ref[0, step, part] = line
            return carry

        return emit

    lax.fori_loop(0, SLOTS, fill, 0, unroll=4)
    half = LOCAL // 2
    for begin, half_ref in zip((0, half), half_refs or (None, None)):
        lax.fori_loop(0, half, emit_from(begin, half_ref), 0, unroll=4)


def unpack(parcels, in_halves):
    shape = jax.ShapeDtypeStruct((1, LOCAL, 2, SLOTS, SIDE), BF16)
    half = jax.ShapeDtypeStruct((1, LOCAL // 2, 2, SLOTS, SIDE), BF16)
    return pl.pallas_call(
        unpack_kernel,
        out_shape=[shape, half, half] if in_halves else [shape],
        scratch_shapes=[pltpu.VMEM((2 * LOCAL * SLOTS, SIDE), F32)],
        compiler_params=pltpu.CompilerParams(vmem_limit_bytes=24 * MIB),
        cost_estimate=pl.CostEstimate(flops=0, bytes_accessed=8 * MIB, transcendentals=0),
        name="unpack",
    )(parcels)


def correlate_kernel(*refs):
    in_refs, refs = refs[:-13], refs[-13:]
    w1_ref, w2_from, w3_from, w4_ref, out_ref, wide, mid, back, tail, w2_ref, w3_ref = refs[:-2]
    fetches = [
        pltpu.make_async_copy(w2_from, w2_ref, refs[-2]),
        pltpu.make_async_copy(w3_from, w3_ref, refs[-1]),
    ]
    for fetch in fetches:
        fetch.start()
    chunk = 2 * LOCAL

    def fill(source, carry):
        start = pl.multiple_of(source * chunk, chunk)
        for which, ref in enumerate(in_refs):
            block = ref[source, 0].reshape(chunk, SIDE)
            wide[which, pl.ds(start, chunk), :] = block.astype(F32)
        return carry

    def first(n, carry):
        cols = [
            jnp.concatenate(
                [
                    wide[which, pl.ds(part * LOCAL + n, SLOTS, stride=chunk), :]
                    for part in range(2)
                ],
                axis=0,
            ).astype(BF16)
            for which in range(2)
        ]
        x = jnp.concatenate(cols, axis=1)
        y = mm(w1_ref[...], jnp.concatenate([x, x], axis=0))
        start = pl.multiple_of(n * 2 * OUTER, 2 * OUTER)
        mid[0, pl.ds(start, 2 * OUTER), :] = y[:, :SIDE]
        mid[1, pl.ds(start, 2 * OUTER), :] = y[:, SIDE:]
        return carry

    def middle(k, carry):
        cols = [
            jnp.concatenate(
                [
                    mid[which, pl.ds(part * OUTER + k, LOCAL, stride=2 * OUTER), :]
                    for part in range(2)
                ],
                axis=0,
            )
            for which in range(2)
        ]
        high, low = split(jnp.concatenate(cols, axis=1))
        z = mm(w2_ref[k], jnp.concatenate([high, high, low], axis=0))
        g_re, g_im = z[:LOCAL, :SIDE], z[LOCAL:, :SIDE]
        h_re, h_im = z[:LOCAL, SIDE:], z[LOCAL:, SIDE:]
        product = jnp.concatenate([g_re * h_re + g_im * h_im, g_im * h_re - g_re * h_im], axis=0)
        high, low = split(product)
        start = pl.multiple_of(k * chunk, chunk)
        back[pl.ds(start, chunk), :] = mm(w3_ref[k], jnp.concatenate([high, high, low], axis=0))
        return carry

    def last(pair, carry):
        lines = [
            jnp.concatenate(
                [
                    back[pl.ds(part * LOCAL + 2 * pair + which, OUTER, stride=chunk), :]
                    for part in range(2)
                ],
                axis=0,
            )
            for which in range(2)
        ]
        high, low = split(jnp.concatenate(lines, axis=1))
        both = mm(w4_ref[...], high)
        y = both[:OUTER] + both[OUTER:] + mm(w4_ref[:OUTER, :], low)
        start = pl.multiple_of(pair * 2 * OUTER, 2 * OUTER)
        tail[pl.ds(start, OUTER), :] = y[:, :SIDE]
        tail[pl.ds(start + OUTER, OUTER), :] = y[:, SIDE:]
        return carry

    def emit(slot, carry):
        for part in range(2):
            line = tail[pl.ds(part * SLOTS + slot, LOCAL, stride=OUTER), :]
            out_ref[slot, part * LOCAL : (part + 1) * LOCAL, :] = line.astype(BF16)
        return carry

    lax.fori_loop(0, SLOTS, fill, 0, unroll=4)
    lax.fori_loop(0, LOCAL, first, 0, unroll=U1)
    for fetch in fetches:
        fetch.wait()
    lax.fori_loop(0, OUTER, middle, 0, unroll=U2)
    lax.fori_loop(0, LOCAL // 2, last, 0, unroll=U4)
    lax.fori_loop(0, SLOTS, emit, 0, unroll=8)


U1, U2, U4 = 4, 32, 4


def correlate(less, greater, tables):
    def parcel(place):
        return pl.BlockSpec((SLOTS, 1, 2, LOCAL, SIDE), lambda s: (0, place, 0, 0, 0))

    vmem = pl.BlockSpec(memory_space=pltpu.VMEM)
    return pl.pallas_call(
        correlate_kernel,
        grid=(1,),
        out_shape=jax.ShapeDtypeStruct((SLOTS, 2 * LOCAL, SIDE), BF16),
        in_specs=[parcel(less[1]), parcel(greater[1]), vmem]
        + [pl.BlockSpec(memory_space=pl.ANY)] * 2
        + [vmem],
        scratch_shapes=[
            pltpu.VMEM((2, ENERGIES * 2, SIDE), F32),
            pltpu.VMEM((2, LOCAL * 2 * OUTER, SIDE), F32),
            pltpu.VMEM((OUTER * 2 * LOCAL, SIDE), F32),
            pltpu.VMEM((LOCAL * OUTER, SIDE), F32),
            pltpu.VMEM(tables[1].shape, BF16),
            pltpu.VMEM(tables[2].shape, BF16),
            pltpu.SemaphoreType.DMA,
            pltpu.SemaphoreType.DMA,
        ],
        compiler_params=pltpu.CompilerParams(vmem_limit_bytes=60 * MIB),
        cost_estimate=pl.CostEstimate(
            flops=12 * 10**9, bytes_accessed=40 * MIB, transcendentals=0
        ),
        name="correlate",
    )(less[0], greater[0], *tables)


SPAN = 8
GROUP = 4


def screen_kernel(*refs):
    left_ref, right_ref = refs[6:8]
    out_ref, polar_ref = refs[-2:]

    def step(group, carry):
        rows = []
        for inner in range(GROUP):
            n = group * GROUP + inner
            fields = []
            for which in range(3):
                top, bottom = refs[2 * which : 2 * which + 2]
                blocks = [
                    jnp.concatenate([top[0, n, part], bottom[0, n, part]], axis=0)
                    for part in range(2)
                ]
                if which == 1:
                    polar_ref[0, n, 0] = blocks[0]
                    polar_ref[0, n, 1] = blocks[1]
                both = jnp.concatenate(blocks, axis=1)
                fields.append(mm(left_ref[which], both).astype(BF16))
            for part in range(2):
                cols = slice(part * SIDE, (part + 1) * SIDE)
                rows.append(jnp.concatenate([field[:, cols] for field in fields], axis=1))
        result = mm(jnp.concatenate(rows, axis=0), right_ref[...]).astype(BF16)
        for inner in range(GROUP):
            for part in range(2):
                start = (2 * inner + part) * SIDE
                block = result[start : start + SIDE]
                out_ref[0, group * GROUP + inner, part] = block[:, :SIDE]
                out_ref[0, group * GROUP + inner, 2 + part] = block[:, SIDE:]
        return carry

    lax.fori_loop(0, SPAN // GROUP, step, 0, unroll=True)


def screen(fields, left, right, half, results):
    steps = LOCAL // (2 * SPAN)

    def spec(parts):
        return pl.BlockSpec((1, SPAN, parts, SIDE, SIDE), lambda s: (0, s + half * steps, 0, 0, 0))

    def field_spec(field):
        first = half * steps if field.shape[1] == LOCAL else 0
        return pl.BlockSpec((1, SPAN, 2, SLOTS, SIDE), lambda s: (0, s + first, 0, 0, 0))

    return pl.pallas_call(
        screen_kernel,
        grid=(steps,),
        out_shape=[
            jax.ShapeDtypeStruct((1, LOCAL, 4, SIDE, SIDE), BF16),
            jax.ShapeDtypeStruct((1, LOCAL, 2, SIDE, SIDE), BF16),
        ],
        in_specs=[field_spec(field) for field in fields]
        + [
            pl.BlockSpec(left.shape, lambda s: (0, 0, 0)),
            pl.BlockSpec(right.shape, lambda s: (0, 0)),
        ]
        + [pl.BlockSpec(memory_space=pl.ANY)] * len(results),
        out_specs=[spec(4), spec(2)],
        input_output_aliases={8 + i: i for i in range(len(results))},
        compiler_params=pltpu.CompilerParams(vmem_limit_bytes=63 * MIB),
        cost_estimate=pl.CostEstimate(
            flops=2 * 10**9, bytes_accessed=10 * MIB, transcendentals=0
        ),
        name="screen",
    )(*fields, left, right, *results)


def from_below(cells):
    ends = lax.axis_size("len") - 1
    return lax.ppermute(cells, "len", [(i, i + 1) for i in range(ends)])


def from_above(cells):
    ends = lax.axis_size("len") - 1
    return lax.ppermute(cells, "len", [(i + 1, i) for i in range(ends)])


def swap(cells, first):
    ends = lax.axis_size("len") - 1
    pairs = [(i, i + 1) for i in range(first, ends, 2)]
    return lax.ppermute(cells, "len", pairs + [(j, i) for i, j in pairs])


def exchange(parcels):
    return lax.all_to_all(parcels, "eng", split_axis=0, concat_axis=0, tiled=True)


def coefficients(coulomb):
    own_diag, own_up = coulomb[0, 0], coulomb[0, 1]
    prev_up = from_below(coulomb[:, 1])[0]
    next_diag = from_above(coulomb[:, 0])[0]
    below = (prev_up.T, jnp.concatenate([prev_up, jnp.zeros_like(prev_up)], axis=1))
    above = (own_up, jnp.concatenate([own_up.T, next_diag], axis=1))
    odd = lax.axis_index("len") % 2 == 1
    one, two = [
        [jnp.where(odd, x, y) for x, y in zip(*order)]
        for order in ((below, above), (above, below))
    ]
    left = jnp.stack([one[0], own_diag, two[0]])
    middle = jnp.concatenate([own_diag, own_up], axis=1)
    right = jnp.concatenate([one[1], middle, two[1]], axis=0)
    return left, right


def forward(less, greater, tables, apart):
    if apart:
        pair = [(exchange(pack([(field, 0)])), 0) for field in (less, greater)]
    else:
        both = exchange(pack([(less, 0), (greater, 0)]))
        pair = [(both, 0), (both, 1)]
    late = exchange(pack([(less, 1), (greater, 1)]))
    first = exchange(correlate(*pair, tables))
    return first, correlate((late, 0), (late, 1), tables)


def body(less_green, greater_green, coulomb):
    tables = [jnp.asarray(table) for table in TABLES]
    first, second = lax.cond(
        lax.axis_index("len") % 2 == 0,
        lambda x, y: forward(x, y, tables, False),
        lambda x, y: forward(x, y, tables, True),
        less_green,
        greater_green,
    )
    (top,) = unpack(first, False)
    top, left, right = lax.optimization_barrier((top, *coefficients(coulomb)))
    bottom, *halves = unpack(exchange(second), True)
    one = [swap(top, 0), swap(bottom, 0)]
    two = [swap(top, 1), *[swap(rows, 1) for rows in halves]]
    results = ()
    for half in range(2):
        fields = (*one, top, bottom, two[0], two[1 + half])
        results = screen(fields, left, right, half, results)
    screened, polar = results
    return polar, screened


def solution(mesh):
    in_specs = (
        P("len", "eng", None, None, None),
        P("len", "eng", None, None, None),
        P("len", None, None, None),
    )
    out_specs = (P("len", "eng", None, None, None), P("len", "eng", None, None, None))
    return jax.shard_map(body, mesh=mesh, in_specs=in_specs, out_specs=out_specs, check_vma=False)
```
